256 devices in a mesh: ent: 64 (over z, x, core), rep: 4 (over y).
Axes of the slice: x: 4, y: 4, z: 8, core: 2. Of those that a mesh axis runs over, the one named last changes fastest.
Arguments:
- entity_table: float32 [65536, 400], P('ent'), may hold values from -2.5 to 2.5
- relation_table: bfloat16 [5120, 400], replicated, may hold values from -5 to 5
- head_row: int32 [64, 4, 4, 256], P('ent', 'rep'), may hold values from 0 to 1023
- relation: int32 [64, 4, 4, 256], P('ent', 'rep'), may hold values from 0 to 5119
- tail_owner: int32 [64, 4, 4, 256, 1], P('ent', 'rep'), may hold values from 0 to 63; in each aligned block of 256 rows (0 to 255, 256 to 511, ..., all dimensions but the last counted through in order) at most 6 rows name the same one
- tail_row: int32 [64, 4, 4, 256], P('ent', 'rep'), may hold values from 0 to 1023
- live_blocks: int32 [64, 4, 4], P('ent', 'rep'), may hold values from 1 to 2, as said below
- negative_row: int32 [1024], P('ent'), may hold values from 0 to 1023
Outputs:
- entity_grad: float32 [65536, 400], P('ent')
- relation_grad: float32 [5120, 400], P(('ent', 'rep'))
The draws below stay inside these ranges and needn't reach their ends.
Inputs may be any that keep to these rules, and one draw needn't show every extreme that they name: `tail_owner`: among the 256 slots of one bucket pair of one device, at most 6 name the same partition, counted over all slots, live or not. `live_blocks`: slots at or beyond 128 times this count hold no edge.
All inputs are finite; a program needn't handle non-finite values.
Results may differ from the reference program's by a relative error of at most 0.0003.
Values sent between devices are 32-bit elements; how exact they have to be, the bound alone decides.
A program may use at most 128 MiB of HBM per device.

```python
import math
import jax
import jax.numpy as jnp
import numpy as np
from jax import lax

D = 400
RELS = 5120
NEG = 1024
SPAN = 128
BUCKETS = 4
EDGES_B = 256
ENT_DEV = 1024
ENT_PARTS = 64
REP_COPIES = 4
ENTITIES = 65536
CAPACITY = 6


def draw_relation(key, part):
    key = jax.random.fold_in(key, 11)
    first_key, second_key, third_key = jax.random.split(key, 3)
    shape = (ENT_PARTS, REP_COPIES, BUCKETS, EDGES_B)
    rows_each = RELS // (ENT_PARTS * REP_COPIES)
    device_flat = jnp.arange(ENT_PARTS, dtype=jnp.int32)[:, None] * REP_COPIES + jnp.arange(REP_COPIES, dtype=jnp.int32)[None, :]
    own_rel = device_flat[:, :, None, None] * rows_each + jax.random.randint(first_key, shape, 0, rows_each)
    other_rel = jax.random.randint(second_key, shape, 0, RELS)
    picker = jax.random.randint(third_key, shape, 0, 2)
    return jnp.where(picker == 1, own_rel, other_rel).astype(jnp.int32)


def draw_live_blocks(key, part):
    key = jax.random.fold_in(key, 23)
    most_blocks = EDGES_B // SPAN
    counts = jax.random.randint(key, (ENT_PARTS, REP_COPIES, BUCKETS), 1, most_blocks + 1)
    counts = counts.at[0, 0, 0].set(most_blocks)
    counts = counts.at[0, 0, 1].set(1)
    return counts.astype(jnp.int32)


def place_ends(array, own_key, smallest, top_value):
    place = [jax.random.randint(jax.random.fold_in(own_key, axis), (), 0, length) for axis, length in enumerate(array.shape)]
    widest = array.shape.index(max(array.shape))
    next_to = place[:widest] + [(place[widest] + 1) % array.shape[widest]] + place[widest + 1:]
    return array.at[tuple(place)].set(smallest).at[tuple(next_to)].set(top_value)


def steps_of(key, shape, pieces, least, high):
    level, own = 1.0, jax.random.fold_in(key, 6)
    for dim, blocks in pieces:
        steps = jnp.exp(jax.random.uniform(jax.random.fold_in(own, dim), (blocks,), jnp.float32, least / len(pieces), high / len(pieces)))
        level = level * jnp.repeat(steps, shape[dim] // blocks).reshape([-1 if axis == dim else 1 for axis in range(len(shape))])
    return level


def deal_out(rng, own, number, rows, number_of, top, bound, slope):
    order = jax.random.permutation(rng, number_of)
    packed, ordinary = load_shares(number_of, rows * top, bound, slope, True), load_shares(number_of, rows * top, bound, slope, False)
    places = jnp.arange(number_of)

    def named(lengths, turn):
        used = int((lengths > 0).sum())
        fixed = max(1, used // 4)
        moved = fixed + (places - fixed + turn * (used - fixed)) % max(1, number_of - fixed)
        return jnp.zeros((number_of,), jnp.int32).at[order[jnp.where(places < fixed, places, moved)]].set(jnp.asarray(lengths, jnp.int32))

    lengths = jnp.where(number % 4 == 0, named(packed, number // 4), named(ordinary, number - number // 4 - 1))
    mixed = jax.random.permutation(jax.random.fold_in(own, 3), number_of)
    source_of, sink = mixed[0:number_of // 2 * 2:2], mixed[1:number_of // 2 * 2:2]
    slack = jnp.minimum(lengths[source_of] - 1, bound - lengths[sink]) // 2
    slack = jnp.where((source_of == order[0]) | (sink == order[0]) | (lengths[sink] == 0), 0, jnp.maximum(slack, 0))
    moved = jax.random.randint(jax.random.fold_in(own, 4), (number_of // 2,), 0, 1 << 20) % (slack + 1)
    lengths = lengths.at[source_of].add(-moved).at[sink].add(moved)
    members = jnp.searchsorted(jnp.cumsum(lengths), jnp.arange(rows * top), side="right").astype(jnp.int32)
    listing = members.reshape(top, rows).T
    listing = listing[jax.random.permutation(jax.random.fold_in(own, 1), rows)]
    turn = jax.random.randint(jax.random.fold_in(own, 2), (rows, 1), 0, top)
    return jnp.take_along_axis(listing, (jnp.arange(top)[None, :] + turn) % top, axis=1)


def load_shares(number_of, total, most, slope, full):
    portions = [(1 << 20) // math.isqrt(standing ** slope) + 1 for standing in range(1, number_of + 1)]
    largest = most if full else min(most, max(-(-total // number_of), total * portions[0] // sum(portions)))
    least = 1 if total - largest >= number_of - 1 else 0
    given, spare = [largest] + [least] * (number_of - 1), total - largest - least * (number_of - 1)
    while spare > 0:
        free = [i for i in range(1, number_of) if given[i] < largest] or [i for i in range(1, number_of) if given[i] < most]
        pool, left = sum([portions[i] for i in free]), spare
        for i in free:
            addition = min(most - given[i], max(1, left * portions[i] // pool), spare)
            given[i] = given[i] + addition
            spare = spare - addition
    return np.array(given)


def scatter_about(rng, shape, width, reach, cuts=(), held_as=jnp.bfloat16):
    result = jax.random.normal(rng, shape, jnp.float32) * width
    if len(cuts) > 0:
        result = steps_of(rng, shape, cuts, -0.22, 0.18) * result
    return jnp.clip(result, min=-reach, max=reach).astype(held_as)


def setup_inputs(seed: int = 0) -> dict:
    key_list = jax.random.split(jax.random.key(seed), 9)
    entity_table = scatter_about(key_list[0], (ENTITIES, D), 0.35, 2.5, ((0, 64),), jnp.float32)
    relation_table = scatter_about(key_list[1], (RELS, D), 1.0, 5.0)
    head_row = place_ends(jax.random.randint(key_list[2], (ENT_PARTS, REP_COPIES, BUCKETS, EDGES_B), 0, ENT_DEV), jax.random.fold_in(key_list[2], 1), 0, ENT_DEV - 1).astype(jnp.int32)
    relation = draw_relation(jax.random.fold_in(key_list[8], 71), 0)
    tail_owner_keys = jax.random.split(jax.random.fold_in(key_list[4], 1), ENT_PARTS * REP_COPIES * BUCKETS * EDGES_B // EDGES_B)
    tail_owner_turns = jax.random.permutation(jax.random.fold_in(key_list[4], 3), ENT_PARTS * REP_COPIES * BUCKETS * EDGES_B // EDGES_B)
    tail_owner = jax.vmap(lambda own, number: deal_out(jax.random.fold_in(key_list[4], 2), own, number, EDGES_B, ENT_PARTS, 1, CAPACITY, 1))(tail_owner_keys, tail_owner_turns).reshape((ENT_PARTS, REP_COPIES, BUCKETS, EDGES_B, 1))
    tail_row = place_ends(jax.random.randint(key_list[5], (ENT_PARTS, REP_COPIES, BUCKETS, EDGES_B), 0, ENT_DEV), jax.random.fold_in(key_list[5], 1), 0, ENT_DEV - 1).astype(jnp.int32)
    live_blocks = draw_live_blocks(jax.random.fold_in(key_list[8], 71), 0)
    negative_row = place_ends(jax.random.randint(key_list[7], (NEG,), 0, ENT_DEV), jax.random.fold_in(key_list[7], 1), 0, ENT_DEV - 1).astype(jnp.int32)
    return {"entity_table": entity_table, "relation_table": relation_table, "head_row": head_row, "relation": relation, "tail_owner": tail_owner, "tail_row": tail_row, "live_blocks": live_blocks, "negative_row": negative_row}


precise = lax.Precision.HIGHEST


def reference(entity_table, relation_table, head_row, relation, tail_owner, tail_row, live_blocks, negative_row):
    groups = ENT_PARTS * REP_COPIES * BUCKETS
    feature_width = entity_table.shape[1]
    row_offset = jnp.arange(ENT_PARTS, dtype=jnp.int32) * ENT_DEV
    head_ids = (head_row + row_offset[:, None, None, None]).reshape(groups, EDGES_B).astype(jnp.int32)
    tail_ids = (tail_owner[..., 0] * ENT_DEV + tail_row).reshape(groups, EDGES_B).astype(jnp.int32)
    rel_ids = relation.reshape(groups, EDGES_B)
    live_counts = live_blocks.reshape(groups)
    neg_owner = jnp.arange(NEG, dtype=jnp.int32) // (NEG // ENT_PARTS)
    neg_ids = (neg_owner * ENT_DEV + negative_row).astype(jnp.int32)
    negatives = entity_table[neg_ids]
    positions = jnp.arange(EDGES_B, dtype=jnp.int32)

    def bucket_step(state_carry, inputs):
        grad_table, rel_grads, neg_grads = state_carry
        head_idx, tail_idx, rel_idx, live_count = inputs
        live_float = (positions < SPAN * live_count).astype(jnp.float32)
        head_vecs = entity_table[head_idx]
        tail_vecs = entity_table[tail_idx]
        rel_vecs = relation_table[rel_idx].astype(jnp.float32)
        head_rel = head_vecs * rel_vecs
        positive = jnp.sum(head_rel * tail_vecs, axis=1)
        pos_grad = -jax.nn.sigmoid(-positive) * live_float
        scores = jnp.dot(head_rel, negatives.T, precision=precise)
        weights = jax.nn.sigmoid(scores) * (NEG ** -0.5) * live_float[:, None]
        pull_sum = pos_grad[:, None] * tail_vecs + jnp.dot(weights, negatives, precision=precise)
        grad_table = grad_table.at[head_idx].add(rel_vecs * pull_sum)
        grad_table = grad_table.at[tail_idx].add(pos_grad[:, None] * head_rel)
        rel_grads = rel_grads.at[rel_idx].add(head_vecs * pull_sum)
        neg_grads = neg_grads + jnp.dot(weights.T, head_rel, precision=precise)
        return (grad_table, rel_grads, neg_grads), None

    initial = (jnp.zeros(entity_table.shape, jnp.float32), jnp.zeros((RELS, feature_width), jnp.float32), jnp.zeros((NEG, feature_width), jnp.float32))
    finals, ignored = lax.scan(bucket_step, initial, (head_ids, tail_ids, rel_ids, live_counts))
    grad_table, rel_grads, neg_grads = finals
    grad_table = grad_table.at[neg_ids].add(neg_grads)
    return grad_table, rel_grads
```

```python
import functools

import jax
import jax.numpy as jnp
from jax import lax
from jax.experimental import pallas as pl
from jax.experimental.pallas import tpu as pltpu
from jax.sharding import PartitionSpec as P

D = 400
RELS = 5120
NEG = 1024
SPAN = 128
BUCKETS = 4
EDGES_B = 256
ENT_DEV = 1024
ENT_PARTS = 64
CAPACITY = 6
NZ, NX, NC, NY = 8, 4, 2, 4
PAIR = BUCKETS * CAPACITY
SLOTS = ENT_PARTS * PAIR
BLOCK = 256
STEPS = SLOTS // BLOCK
OWN_NEG = NEG // ENT_PARTS
REL_DEV = RELS // (ENT_PARTS * NY)
ROWS_A, ROWS_B = NZ * 12, NZ * 8
BASE_B = NC * NY * NX * ROWS_A

f32, bf16, i32 = jnp.float32, jnp.bfloat16, jnp.int32
VMEM_LIMIT = 48 * 1024 * 1024
MESH = pl.DeviceIdType.MESH


def split(x):
    hi = x.astype(bf16)
    return hi, (x - hi.astype(f32)).astype(bf16)


def nn(a, b):
    return lax.dot_general(a, b, (((1,), (0,)), ((), ())), preferred_element_type=f32)


def nt(a, b):
    return lax.dot_general(a, b, (((1,), (1,)), ((), ())), preferred_element_type=f32)


def tn(a, b):
    return lax.dot_general(a, b, (((0,), (0,)), ((), ())), preferred_element_type=f32)


def picks_lanes(column, width, start=0):
    lanes = lax.broadcasted_iota(i32, (column.shape[0], width), 1) + start
    return jnp.where(lanes == column, 1.0, 0.0).astype(bf16)


def picks_rows(row, height, start):
    rows = lax.broadcasted_iota(i32, (height, row.shape[1]), 0) + start
    return jnp.where(rows == row, 1.0, 0.0).astype(bf16)


def full(shape):
    return pl.BlockSpec(shape, lambda s: (0,) * len(shape))


def blocked(width):
    return pl.BlockSpec((BLOCK, width), lambda s: (s, 0))


def params(**more):
    return pltpu.CompilerParams(vmem_limit_bytes=VMEM_LIMIT, **more)


def cost(gflop, mbytes):
    return pl.CostEstimate(flops=int(gflop * 1e9), bytes_accessed=int(mbytes * 1e6), transcendentals=0)


def gather_heads_body(head, rel, neg, table, rels, h_out, r_out, hr_out, neg_out, hi, lo):
    @pl.when(pl.program_id(0) == 0)
    def _():
        hi[...], lo[...] = split(table[...])
        pick = picks_lanes(neg[...], ENT_DEV)
        neg_out[...] = nt(pick, hi[...]) + nt(pick, lo[...])

    pick = picks_lanes(head[...], ENT_DEV)
    h = nt(pick, hi[...]) + nt(pick, lo[...])
    r = jnp.zeros((BLOCK, D), f32)
    for k in range(RELS // 1024):
        r += nt(picks_lanes(rel[...], 1024, 1024 * k), rels[:, 1024 * k : 1024 * (k + 1)])
    h_out[...] = h
    r_out[...] = r
    hr_out[...] = h * r


def gather_heads(head, rel, neg, table, rels):
    rows = jax.ShapeDtypeStruct((SLOTS, D), f32)
    return pl.pallas_call(
        gather_heads_body,
        grid=(STEPS,),
        in_specs=[blocked(1), blocked(1), full((OWN_NEG, 1)), full((D, ENT_DEV)), full((D, RELS))],
        out_specs=[blocked(D), blocked(D), blocked(D), full((OWN_NEG, D))],
        out_shape=[rows, rows, rows, jax.ShapeDtypeStruct((OWN_NEG, D), f32)],
        scratch_shapes=[pltpu.VMEM((D, ENT_DEV), bf16), pltpu.VMEM((D, ENT_DEV), bf16)],
        compiler_params=params(),
        cost_estimate=cost(9, 20),
        name="gather_heads",
    )(head, rel, neg, table, rels)


def gather_asked_body(asked, table, out, hi, lo):
    @pl.when(pl.program_id(0) == 0)
    def _():
        hi[...], lo[...] = split(table[...])

    pick = picks_lanes(asked[...], ENT_DEV)
    out[...] = nt(pick, hi[...]) + nt(pick, lo[...])


def gather_asked(asked, table):
    return pl.pallas_call(
        gather_asked_body,
        grid=(STEPS,),
        in_specs=[blocked(1), full((D, ENT_DEV))],
        out_specs=blocked(D),
        out_shape=jax.ShapeDtypeStruct((SLOTS, D), f32),
        scratch_shapes=[pltpu.VMEM((D, ENT_DEV), bf16), pltpu.VMEM((D, ENT_DEV), bf16)],
        compiler_params=params(),
        cost_estimate=cost(3, 6),
        name="gather_asked",
    )(asked, table)


def negatives_body(hr, live, negs, pulled, pushed, hi, lo):
    @pl.when(pl.program_id(0) == 0)
    def _():
        hi[...], lo[...] = split(negs[...])
        pushed[...] = jnp.zeros_like(pushed)

    hr_hi, hr_lo = split(hr[...])
    scores = nt(hr_hi, hi[...]) + nt(hr_hi, lo[...]) + nt(hr_lo, hi[...])
    weights = jax.nn.sigmoid(scores) * (NEG**-0.5 * live[...])
    w_hi, w_lo = split(weights)
    pulled[...] = nn(w_hi, hi[...]) + nn(w_hi, lo[...]) + nn(w_lo, hi[...])
    pushed[...] += tn(w_hi, hr_hi) + tn(w_hi, hr_lo) + tn(w_lo, hr_hi)


def negative_terms(hr, live, negs):
    return pl.pallas_call(
        negatives_body,
        grid=(STEPS,),
        in_specs=[blocked(D), blocked(1), full((NEG, D))],
        out_specs=[blocked(D), full((NEG, D))],
        out_shape=[jax.ShapeDtypeStruct((SLOTS, D), f32), jax.ShapeDtypeStruct((NEG, D), f32)],
        scratch_shapes=[pltpu.VMEM((NEG, D), bf16), pltpu.VMEM((NEG, D), bf16)],
        compiler_params=params(),
        cost_estimate=cost(13, 10),
        name="negative_terms",
    )(hr, live, negs)


def positives_body(tail, hr, live, pulled, tail_grad, pull):
    t, e = tail[...], hr[...]
    positive = jnp.sum(e * t, axis=1, keepdims=True)
    gpos = -jax.nn.sigmoid(-positive) * live[...]
    tail_grad[...] = gpos * e
    pull[...] = gpos * t + pulled[...]


def positive_terms(tail, hr, live, pulled):
    rows = jax.ShapeDtypeStruct((SLOTS, D), f32)
    return pl.pallas_call(
        positives_body,
        grid=(STEPS,),
        in_specs=[blocked(D), blocked(D), blocked(1), blocked(D)],
        out_specs=[blocked(D), blocked(D)],
        out_shape=[rows, rows],
        compiler_params=params(),
        cost_estimate=cost(0.01, 16),
        name="positive_terms",
    )(tail, hr, live, pulled)


def relation_body(row, h, pull, out, hi, lo):
    @pl.when(pl.program_id(0) == 0)
    def _():
        hi[...], lo[...] = split(h[...] * pull[...])

    pick = picks_rows(row[...], BLOCK, BLOCK * pl.program_id(0))
    out[...] = nn(pick, hi[...]) + nn(pick, lo[...])


def relation_terms(row, h, pull):
    return pl.pallas_call(
        relation_body,
        grid=(RELS // BLOCK,),
        in_specs=[full((1, SLOTS)), full((SLOTS, D)), full((SLOTS, D))],
        out_specs=blocked(D),
        out_shape=jax.ShapeDtypeStruct((RELS, D), f32),
        scratch_shapes=[pltpu.VMEM((SLOTS, D), bf16), pltpu.VMEM((SLOTS, D), bf16)],
        compiler_params=params(),
        cost_estimate=cost(13, 16),
        name="relation_terms",
    )(row, h, pull)


def transposed(x):
    return jnp.concatenate([x, jnp.zeros((x.shape[0], 512 - D), f32)], axis=1).T[:D]


def head_body(column, r, pull, neg_column, neg, out, hi, lo):
    @pl.when(pl.program_id(0) == 0)
    def _():
        for s in range(STEPS):
            part = slice(s * BLOCK, (s + 1) * BLOCK)
            hi[:, part], lo[:, part] = split(transposed(r[part] * pull[part]))

    start = pl.program_id(0) * BLOCK
    pick = picks_lanes(column[...], BLOCK, start)
    neg_pick = picks_lanes(neg_column[...], BLOCK, start)
    neg_hi, neg_lo = split(neg[...])
    out[0] = nn(hi[...], pick) + nn(lo[...], pick) + tn(neg_hi, neg_pick) + tn(neg_lo, neg_pick)


def head_terms(column, r, pull, neg_column, neg):
    return pl.pallas_call(
        head_body,
        grid=(ENT_DEV // BLOCK,),
        in_specs=[full((SLOTS, 1)), full((SLOTS, D)), full((SLOTS, D)), full((OWN_NEG, 1)), full((OWN_NEG, D))],
        out_specs=pl.BlockSpec((1, D, BLOCK), lambda s: (s, 0, 0)),
        out_shape=jax.ShapeDtypeStruct((ENT_DEV // BLOCK, D, BLOCK), f32),
        scratch_shapes=[pltpu.VMEM((D, SLOTS), bf16), pltpu.VMEM((D, SLOTS), bf16)],
        compiler_params=params(),
        cost_estimate=cost(3, 10),
        name="head_terms",
    )(column, r, pull, neg_column, neg)


def tail_body(column, incoming, heads, out, hi, lo):
    @pl.when(pl.program_id(0) == 0)
    def _():
        for s in range(STEPS):
            part = slice(s * BLOCK, (s + 1) * BLOCK)
            hi[:, part], lo[:, part] = split(transposed(incoming[part]))

    pick = picks_lanes(column[...], BLOCK, pl.program_id(0) * BLOCK)
    out[0] = heads[0] + (nn(hi[...], pick) + nn(lo[...], pick))


def tail_terms(column, incoming, heads):
    chunk = pl.BlockSpec((1, D, BLOCK), lambda s: (s, 0, 0))
    return pl.pallas_call(
        tail_body,
        grid=(ENT_DEV // BLOCK,),
        in_specs=[full((SLOTS, 1)), full((SLOTS, D)), chunk],
        out_specs=chunk,
        out_shape=jax.ShapeDtypeStruct((ENT_DEV // BLOCK, D, BLOCK), f32),
        scratch_shapes=[pltpu.VMEM((D, SLOTS), bf16), pltpu.VMEM((D, SLOTS), bf16)],
        compiler_params=params(),
        cost_estimate=cost(3, 8),
        name="tail_terms",
    )(column, incoming, heads)


def position():
    ent, y = lax.axis_index("ent"), lax.axis_index("rep")
    return lax.div(ent, NX * NC), lax.rem(lax.div(ent, NC), NX), lax.rem(ent, NC), y


def device(z, x, c, y):
    return ((z * NX + x) * NC + c, y)


def ahead(i, k, n):
    return lax.rem(i + k, n)


def along_z(k):
    z, x, c, y = position()
    return device(ahead(z, k, NZ), x, c, y)


def along_x(k):
    z, x, c, y = position()
    return device(z, ahead(x, k, NX), c, y)


def along_y(k):
    z, x, c, y = position()
    return device(z, x, c, ahead(y, k, NY))


def other_core():
    z, x, c, y = position()
    return device(z, x, 1 - c, y)


def meet(peers):
    barrier = pltpu.get_barrier_semaphore()
    for peer in peers:
        pl.semaphore_signal(barrier, inc=1, device_id=peer, device_id_type=MESH)
    pl.semaphore_wait(barrier, len(peers))


def send(src, dst, send_sem, recv_sem, peer):
    copy = pltpu.make_async_remote_copy(
        src_ref=src, dst_ref=dst, send_sem=send_sem, recv_sem=recv_sem, device_id=peer, device_id_type=MESH
    )
    copy.start()
    return copy


def gather_negatives_body(own, out, send_sem, recv_sem):
    z, x, c, y = position()
    meet([along_z(k) for k in range(1, NZ)] + [along_x(k) for k in range(1, NX)] + [other_core()])
    copies = [send(own, out.at[c, x, z], send_sem.at[k], recv_sem.at[k], along_z(k)) for k in range(1, NZ)]
    out[c, x, z] = own[...]
    for copy in copies:
        copy.wait()
    mine = out.at[c, x]
    copies = [
        send(mine, mine, send_sem.at[NZ + k], recv_sem.at[NZ + k], along_x(k)) for k in range(1, NX)
    ]
    for copy in copies:
        copy.wait()
    mine = out.at[c]
    send(mine, mine, send_sem.at[0], recv_sem.at[0], other_core()).wait()


def gather_negatives(own):
    return pl.pallas_call(
        gather_negatives_body,
        in_specs=[pl.BlockSpec(memory_space=pltpu.VMEM)],
        out_specs=pl.BlockSpec(memory_space=pltpu.VMEM),
        out_shape=jax.ShapeDtypeStruct((NC, NX, NZ, OWN_NEG, D), f32),
        scratch_shapes=[pltpu.SemaphoreType.DMA((NZ + NX,)), pltpu.SemaphoreType.DMA((NZ + NX,))],
        compiler_params=params(collective_id=0),
        cost_estimate=cost(0, 40),
        name="gather_negatives",
    )(own)


def sum_negatives_body(part, out, at_core, at_x, at_z, send_sem, recv_sem):
    z, x, c, y = position()
    meet([along_z(k) for k in range(1, NZ)] + [along_x(k) for k in range(1, NX)] + [other_core()])
    first = send(part.at[1 - c], at_core, send_sem.at[0], recv_sem.at[0], other_core())
    first.wait_recv()
    at_core[...] += part[c]
    copies = [
        send(at_core.at[ahead(x, k, NX)], at_x.at[k], send_sem.at[NZ + k], recv_sem.at[NZ + k], along_x(k))
        for k in range(1, NX)
    ]
    for copy in copies:
        copy.wait_recv()
    at_x[0] = at_core[x] + at_x[1] + at_x[2] + at_x[3]
    later = [
        send(at_x.at[0, ahead(z, k, NZ)], at_z.at[k], send_sem.at[k], recv_sem.at[k], along_z(k))
        for k in range(1, NZ)
    ]
    total = at_x[0, z]
    for k in range(1, NZ):
        later[k - 1].wait_recv()
        total += at_z[k]
    out[...] = total
    for copy in [first] + copies + later:
        copy.wait_send()


def sum_negatives(part):
    return pl.pallas_call(
        sum_negatives_body,
        in_specs=[pl.BlockSpec(memory_space=pltpu.VMEM)],
        out_specs=pl.BlockSpec(memory_space=pltpu.VMEM),
        out_shape=jax.ShapeDtypeStruct((OWN_NEG, D), f32),
        scratch_shapes=[
            pltpu.VMEM((NX, NZ, OWN_NEG, D), f32),
            pltpu.VMEM((NX, NZ, OWN_NEG, D), f32),
            pltpu.VMEM((NZ, OWN_NEG, D), f32),
            pltpu.SemaphoreType.DMA((NZ + NX,)),
            pltpu.SemaphoreType.DMA((NZ + NX,)),
        ],
        compiler_params=params(collective_id=1),
        cost_estimate=cost(0, 40),
        name="sum_negatives",
    )(part)


class Half:
    def __init__(self, dense, base, rows, m1, m2, along1, along2, acc, far, near, last, sems, first_sem):
        self.dense, self.base, self.rows, self.m1, self.m2 = dense, base, rows, m1, m2
        self.along1, self.along2 = along1, along2
        self.acc, self.far, self.near, self.last = acc, far, near, last
        self.sems, self.first_sem, self.copies = sems, first_sem, {}

    def chunk(self, core, o):
        start = self.base + (core * 4 + ahead(self.m1, o, 4)) * 4 * self.rows
        return pl.ds(pl.multiple_of(start, 8), 4 * self.rows)

    def start(self, name, src, dst, peer):
        index = self.first_sem + len(self.copies)
        self.copies[name] = send(src, dst, self.sems[0].at[index], self.sems[1].at[index], peer)

    def got(self, name):
        self.copies[name].wait_recv()

    def start_core(self, c):
        for o in (2, 1, 3, 0):
            self.start(("core", o), self.dense.at[self.chunk(1 - c, o)], self.acc.at[o], other_core())

    def add_core(self, c, o):
        self.got(("core", o))
        self.acc[o] += self.dense[self.chunk(c, o)]

    def ring_far(self, c):
        two = 2 * self.rows
        self.add_core(c, 2)
        self.start("far right", self.acc.at[2, :two], self.far.at[0], self.along1(1))
        self.start("far left", self.acc.at[2, two:], self.far.at[1], self.along1(3))

    def ring_early(self, c):
        two = 2 * self.rows
        self.add_core(c, 1)
        self.start("early right", self.acc.at[1, two:], self.near.at[0, two:], self.along1(1))
        self.add_core(c, 3)
        self.start("early left", self.acc.at[3, :two], self.near.at[1, :two], self.along1(3))
        self.add_core(c, 0)

    def ring_near(self):
        two = 2 * self.rows
        self.got("far right")
        self.acc[1, :two] += self.far[0]
        self.start("near right", self.acc.at[1, :two], self.near.at[0, :two], self.along1(1))
        self.got("far left")
        self.acc[3, two:] += self.far[1]
        self.start("near left", self.acc.at[3, two:], self.near.at[1, two:], self.along1(3))

    def second(self):
        for name in ("early right", "early left", "near right", "near left"):
            self.got(name)
        self.acc[0] += self.near[0] + self.near[1]
        for k in (2, 1, 3):
            part = pl.ds(pl.multiple_of(ahead(self.m2, k, 4) * self.rows, 8), self.rows)
            self.start(("second", k), self.acc.at[0, part], self.last.at[k], self.along2(k))

    def result(self):
        total = self.acc[0, pl.ds(pl.multiple_of(self.m2 * self.rows, 8), self.rows)]
        for k in (1, 3, 2):
            self.got(("second", k))
            total += self.last[k]
        return total

    def finish(self):
        for copy in self.copies.values():
            copy.wait_send()


def sum_relations_body(
    dense, out, acc_a, far_a, near_a, last_a, acc_b, far_b, near_b, last_b, going, arrived, send_sem, recv_sem
):
    z, x, c, y = position()
    meet(
        [along_z(k) for k in range(1, NZ)]
        + [along_x(k) for k in range(1, NX)]
        + [along_y(k) for k in range(1, NY)]
        + [other_core()]
    )
    sems = (send_sem, recv_sem)
    a = Half(dense, 0, ROWS_A, y, x, along_y, along_x, acc_a, far_a, near_a, last_a, sems, 0)
    b = Half(dense, BASE_B, ROWS_B, x, y, along_x, along_y, acc_b, far_b, near_b, last_b, sems, 16)
    a.start_core(c)
    b.start_core(c)
    a.ring_far(c)
    a.ring_early(c)
    b.ring_far(c)
    b.ring_early(c)
    a.ring_near()
    b.ring_near()
    b.second()
    a.second()
    sum_b = b.result()
    sum_a = a.result()
    for i in range(NZ):
        going[i, 0:8] = sum_a[8 * i : 8 * i + 8]
        going[i, 8:16] = sum_b[8 * i : 8 * i + 8]
        going[i, 16:20] = sum_a[8 * NZ + 4 * i : 8 * NZ + 4 * i + 4]
        going[i, 20:24] = jnp.zeros((4, D), f32)
    copies = [
        send(going.at[ahead(z, k, NZ)], arrived.at[k], send_sem.at[32 + k], recv_sem.at[32 + k], along_z(k))
        for k in range(1, NZ)
    ]
    total = going[z]
    for k in range(1, NZ):
        copies[k - 1].wait_recv()
        total += arrived[k]
    out[...] = total[:REL_DEV]
    a.finish()
    b.finish()
    for copy in copies:
        copy.wait_send()


def sum_relations(dense):
    def buffers(rows):
        return [
            pltpu.VMEM((4, 4 * rows, D), f32),
            pltpu.VMEM((2, 2 * rows, D), f32),
            pltpu.VMEM((2, 4 * rows, D), f32),
            pltpu.VMEM((4, rows, D), f32),
        ]

    return pl.pallas_call(
        sum_relations_body,
        in_specs=[pl.BlockSpec(memory_space=pltpu.VMEM)],
        out_specs=pl.BlockSpec(memory_space=pltpu.VMEM),
        out_shape=jax.ShapeDtypeStruct((REL_DEV, D), f32),
        scratch_shapes=buffers(ROWS_A)
        + buffers(ROWS_B)
        + [
            pltpu.VMEM((NZ, 24, D), f32),
            pltpu.VMEM((NZ, 24, D), f32),
            pltpu.SemaphoreType.DMA((32 + NZ,)),
            pltpu.SemaphoreType.DMA((32 + NZ,)),
        ],
        compiler_params=params(collective_id=2),
        cost_estimate=cost(0, 150),
        name="sum_relations",
    )(dense)


def sum_copies_body(part, out, far, near, send_sem, recv_sem):
    y = lax.axis_index("rep")
    right, left = along_y(1), along_y(3)
    meet([right, left])
    at = [ahead(y, o, 4) for o in range(4)]
    top, low = slice(0, D // 2), slice(D // 2, D)

    def start(index, src, dst, peer):
        return send(src, dst, send_sem.at[index], recv_sem.at[index], peer)

    def chunk(o, rows):
        return out.at[rows, pl.ds(pl.multiple_of(at[o] * BLOCK, BLOCK), BLOCK)]

    far_right = start(0, part.at[at[2], top], far.at[0], right)
    far_left = start(1, part.at[at[2], low], far.at[1], left)
    early_right = start(2, part.at[at[1], low], near.at[0, low], right)
    early_left = start(3, part.at[at[3], top], near.at[1, top], left)
    far_right.wait_recv()
    far[0] += part[at[1], top]
    near_right = start(4, far.at[0], near.at[0, top], right)
    far_left.wait_recv()
    far[1] += part[at[3], low]
    near_left = start(5, far.at[1], near.at[1, low], left)

    early_left.wait_recv()
    near_right.wait_recv()
    chunk(0, top)[...] = part[at[0], top] + near[0, top] + near[1, top]
    own_top_right = start(6, chunk(0, top), chunk(0, top), right)
    own_top_left = start(7, chunk(0, top), chunk(0, top), left)
    early_right.wait_recv()
    near_left.wait_recv()
    chunk(0, low)[...] = part[at[0], low] + near[0, low] + near[1, low]
    own_low_left = start(8, chunk(0, low), chunk(0, low), left)
    own_low_right = start(9, chunk(0, low), chunk(0, low), right)
    own_top_right.wait_recv()
    next_right = start(10, chunk(3, top), chunk(3, top), right)
    own_low_left.wait_recv()
    next_left = start(11, chunk(1, low), chunk(1, low), left)
    for copy in (own_top_left, own_low_right, next_right, next_left):
        copy.wait_recv()
    for copy in (far_right, far_left, early_right, early_left, near_right, near_left):
        copy.wait_send()
    for copy in (own_top_right, own_top_left, own_low_left, own_low_right, next_right, next_left):
        copy.wait_send()


def sum_copies(part):
    return pl.pallas_call(
        sum_copies_body,
        in_specs=[pl.BlockSpec(memory_space=pltpu.VMEM)],
        out_specs=pl.BlockSpec(memory_space=pltpu.VMEM),
        out_shape=jax.ShapeDtypeStruct((D, ENT_DEV), f32),
        scratch_shapes=[
            pltpu.VMEM((2, D // 2, BLOCK), f32),
            pltpu.VMEM((2, D, BLOCK), f32),
            pltpu.SemaphoreType.DMA((12,)),
            pltpu.SemaphoreType.DMA((12,)),
        ],
        compiler_params=params(collective_id=3),
        cost_estimate=cost(0, 80),
        name="sum_copies",
    )(part)


def place_edges(head_row, relation, tail_owner, tail_row, live_blocks):
    live = jnp.arange(EDGES_B, dtype=i32)[None, :] < SPAN * live_blocks[:, None]
    before = jnp.arange(EDGES_B)[None, :] < jnp.arange(EDGES_B)[:, None]
    same = tail_owner[:, :, None] == tail_owner[:, None, :]
    rank = jnp.sum((same & before[None]).astype(i32), axis=2)
    key = jnp.where(live, tail_owner * CAPACITY + rank, -1)
    slots = jnp.arange(ENT_PARTS * CAPACITY, dtype=i32)
    match = key[:, None, :] == slots[None, :, None]

    def placed(values):
        found = jnp.sum(jnp.where(match, values[:, None, :] + 1, 0), axis=2) - 1
        found = found.reshape(BUCKETS, ENT_PARTS, CAPACITY)
        return jnp.transpose(found, (1, 0, 2)).reshape(ENT_PARTS, PAIR)

    ends = placed(head_row * ENT_DEV + tail_row)
    taken = ends >= 0
    heads = jnp.where(taken, lax.shift_right_arithmetic(ends, 10), -1)
    tails = jnp.where(taken, ends & (ENT_DEV - 1), -1)
    return heads, placed(relation), tails


def dense_rows(rel):
    owner, j = rel // REL_DEV, rel % REL_DEV
    y, ent = owner % NY, owner // NY
    c, x, z = ent % NC, (ent // NC) % NX, ent // (NC * NX)
    in_a = (c * NY + y) * NX + x
    in_b = BASE_B + ((c * NX + x) * NY + y) * ROWS_B + z * 8 + j - 8
    row_a = in_a * ROWS_A + z * 8 + j
    row_c = in_a * ROWS_A + NZ * 8 + z * 4 + j - 16
    return jnp.where(rel < 0, -1, jnp.where(j < 8, row_a, jnp.where(j < 16, in_b, row_c)))


def shards(entity_table, relation_table, head_row, relation, tail_owner, tail_row, live_blocks, negative_row):
    table, rels = entity_table.T, relation_table.T
    heads, rel, tails = place_edges(
        head_row[0, 0], relation[0, 0], tail_owner[0, 0, :, :, 0], tail_row[0, 0], live_blocks[0, 0]
    )
    asked = lax.all_to_all(tails, "ent", split_axis=0, concat_axis=0, tiled=True)
    head_column = heads.reshape(SLOTS, 1)
    live = (head_column >= 0).astype(f32)
    neg_column = negative_row.reshape(OWN_NEG, 1)
    h, r, hr, own_neg = gather_heads(head_column, rel.reshape(SLOTS, 1), neg_column, table, rels)
    asked_column = asked.reshape(SLOTS, 1)
    rows = gather_asked(asked_column, table)
    fetched = lax.all_to_all(
        rows.reshape(ENT_PARTS, PAIR, D), "ent", split_axis=0, concat_axis=0, tiled=True
    )
    negs = gather_negatives(own_neg).reshape(NEG, D)
    pulled, pushed = negative_terms(hr, live, negs)
    neg_grad = sum_negatives(pushed.reshape(NC, NX, NZ, OWN_NEG, D))
    tail_grad, pull = positive_terms(fetched.reshape(SLOTS, D), hr, live, pulled)
    incoming = lax.all_to_all(
        tail_grad.reshape(ENT_PARTS, PAIR, D), "ent", split_axis=0, concat_axis=0, tiled=True
    )
    dense = relation_terms(dense_rows(rel).reshape(1, SLOTS), h, pull)
    rel_grad = sum_relations(dense)
    head_part = head_terms(head_column, r, pull, neg_column, neg_grad)
    part = tail_terms(asked_column, incoming.reshape(SLOTS, D), head_part)
    return sum_copies(part).T, rel_grad


def solution(mesh):
    placed = (
        P("ent", None),
        P(),
        P("ent", "rep", None, None),
        P("ent", "rep", None, None),
        P("ent", "rep", None, None, None),
        P("ent", "rep", None, None),
        P("ent", "rep", None),
        P("ent"),
    )
    return jax.shard_map(
        shards,
        mesh=mesh,
        in_specs=placed,
        out_specs=(P("ent", None), P(("ent", "rep"), None)),
        check_vma=False,
    )
```

```python
import functools

import jax
import jax.numpy as jnp
from jax import lax
from jax.experimental import pallas as pl
from jax.experimental.pallas import tpu as pltpu
from jax.sharding import PartitionSpec as P

D = 400
RELS = 5120
NEG = 1024
SPAN = 128
BUCKETS = 4
EDGES_B = 256
ENT_DEV = 1024
ENT_PARTS = 64
CAPACITY = 6
NZ, NX, NC, NY = 8, 4, 2, 4
PAIR = BUCKETS * CAPACITY
SLOTS = ENT_PARTS * PAIR
BLOCK = 256
STEPS = SLOTS // BLOCK
PACKED = 80
GROUP = 16
GROUP_ROWS = GROUP * PAIR
GROUPS = ENT_PARTS // GROUP
OWN_NEG = NEG // ENT_PARTS
REL_DEV = RELS // (ENT_PARTS * NY)
ROWS_A, ROWS_B = NZ * 12, NZ * 8
BASE_B = NC * NY * NX * ROWS_A

f32, bf16, i32 = jnp.float32, jnp.bfloat16, jnp.int32
VMEM_LIMIT = 48 * 1024 * 1024
MESH = pl.DeviceIdType.MESH


def split(x):
    hi = x.astype(bf16)
    return hi, (x - hi.astype(f32)).astype(bf16)


def nn(a, b):
    return lax.dot_general(a, b, (((1,), (0,)), ((), ())), preferred_element_type=f32)


def nt(a, b):
    return lax.dot_general(a, b, (((1,), (1,)), ((), ())), preferred_element_type=f32)


def tn(a, b):
    return lax.dot_general(a, b, (((0,), (0,)), ((), ())), preferred_element_type=f32)


def pack(x):
    parts = [x[:, 128 * i : 128 * (i + 1)].reshape(GROUP, PAIR, 128) for i in range(3)]
    rest = jnp.concatenate([x[:, 384:], jnp.zeros((GROUP_ROWS, 512 - D), f32)], axis=1).reshape(GROUP, PAIR, 128)
    tile = rest[:, 0:8].reshape(GROUP * 8, 128)
    for i in (1, 2):
        tile += pltpu.roll(rest[:, 8 * i : 8 * (i + 1)].reshape(GROUP * 8, 128), 16 * i, 1)
    return jnp.concatenate(parts + [tile.reshape(GROUP, 8, 128)], axis=1)


def unpack(p):
    parts = [p[:, PAIR * i : PAIR * (i + 1)].reshape(GROUP_ROWS, 128) for i in range(3)]
    tile = p[:, 3 * PAIR :].reshape(GROUP * 8, 128)
    rest = [tile, pltpu.roll(tile, 112, 1), pltpu.roll(tile, 96, 1)]
    rest = jnp.concatenate([x.reshape(GROUP, 8, 128) for x in rest], axis=1).reshape(GROUP_ROWS, 128)
    return jnp.concatenate(parts + [rest[:, : D - 384]], axis=1)


def picks_lanes(column, width, start=0):
    lanes = lax.broadcasted_iota(i32, (column.shape[0], width), 1) + start
    return jnp.where(lanes == column, 1.0, 0.0).astype(bf16)


def picks_rows(row, height, start):
    rows = lax.broadcasted_iota(i32, (height, row.shape[1]), 0) + start
    return jnp.where(rows == row, 1.0, 0.0).astype(bf16)


def full(shape):
    return pl.BlockSpec(shape, lambda s: (0,) * len(shape))


def blocked(width):
    return pl.BlockSpec((BLOCK, width), lambda s: (s, 0))


def grouped(width):
    return pl.BlockSpec((GROUP_ROWS, width), lambda s: (s, 0))


packed_block = pl.BlockSpec((GROUP, PACKED, 128), lambda s: (s, 0, 0))
packed_rows = jax.ShapeDtypeStruct((ENT_PARTS, PACKED, 128), f32)


def params(**more):
    return pltpu.CompilerParams(vmem_limit_bytes=VMEM_LIMIT, **more)


def cost(gflop, mbytes):
    return pl.CostEstimate(flops=int(gflop * 1e9), bytes_accessed=int(mbytes * 1e6), transcendentals=0)


def gather_heads_body(head, rel, table, rels, h_out, r_out, hr_out, hi, lo):
    @pl.when(pl.program_id(0) == 0)
    def _():
        hi[...], lo[...] = split(table[...])

    pick = picks_lanes(head[...], ENT_DEV)
    h = nt(pick, hi[...]) + nt(pick, lo[...])
    r = jnp.zeros((BLOCK, D), f32)
    for k in range(RELS // 1024):
        r += nt(picks_lanes(rel[...], 1024, 1024 * k), rels[:, 1024 * k : 1024 * (k + 1)])
    h_out[...] = h
    r_out[...] = r
    hr_out[...] = h * r


def gather_heads(head, rel, table, rels):
    rows = jax.ShapeDtypeStruct((SLOTS, D), f32)
    return pl.pallas_call(
        gather_heads_body,
        grid=(STEPS,),
        in_specs=[blocked(1), blocked(1), full((D, ENT_DEV)), full((D, RELS))],
        out_specs=[blocked(D), blocked(D), blocked(D)],
        out_shape=[rows, rows, rows],
        scratch_shapes=[pltpu.VMEM((D, ENT_DEV), bf16), pltpu.VMEM((D, ENT_DEV), bf16)],
        compiler_params=params(),
        cost_estimate=cost(9, 20),
        name="gather_heads",
    )(head, rel, table, rels)


def gather_asked_body(asked, table, out, hi, lo):
    @pl.when(pl.program_id(0) == 0)
    def _():
        hi[...], lo[...] = split(table[...])

    pick = picks_lanes(asked[...], ENT_DEV)
    out[...] = pack(nt(pick, hi[...]) + nt(pick, lo[...]))


def gather_asked(asked, table):
    return pl.pallas_call(
        gather_asked_body,
        grid=(GROUPS,),
        in_specs=[grouped(1), full((D, ENT_DEV))],
        out_specs=packed_block,
        out_shape=packed_rows,
        scratch_shapes=[pltpu.VMEM((D, ENT_DEV), bf16), pltpu.VMEM((D, ENT_DEV), bf16)],
        compiler_params=params(),
        cost_estimate=cost(3, 6),
        name="gather_asked",
    )(asked, table)


def negatives_body(hr, live, negs, pulled, pushed, hi, lo):
    @pl.when(pl.program_id(0) == 0)
    def _():
        hi[...], lo[...] = split(negs[...])
        pushed[...] = jnp.zeros_like(pushed)

    hr_hi, hr_lo = split(hr[...])
    scores = nt(hr_hi, hi[...]) + nt(hr_hi, lo[...]) + nt(hr_lo, hi[...])
    weights = jax.nn.sigmoid(scores) * (NEG**-0.5 * live[...])
    w_hi, w_lo = split(weights)
    pulled[...] = nn(w_hi, hi[...]) + nn(w_hi, lo[...]) + nn(w_lo, hi[...])
    pushed[...] += tn(w_hi, hr_hi) + tn(w_hi, hr_lo) + tn(w_lo, hr_hi)


def negative_terms(hr, live, negs):
    return pl.pallas_call(
        negatives_body,
        grid=(STEPS,),
        in_specs=[blocked(D), blocked(1), full((NEG, D))],
        out_specs=[blocked(D), full((NEG, D))],
        out_shape=[jax.ShapeDtypeStruct((SLOTS, D), f32), jax.ShapeDtypeStruct((NEG, D), f32)],
        scratch_shapes=[pltpu.VMEM((NEG, D), bf16), pltpu.VMEM((NEG, D), bf16)],
        compiler_params=params(),
        cost_estimate=cost(13, 10),
        name="negative_terms",
    )(hr, live, negs)


def positives_body(tail, hr, live, pulled, tail_grad, pull):
    t, e = unpack(tail[...]), hr[...]
    positive = jnp.sum(e * t, axis=1, keepdims=True)
    gpos = -jax.nn.sigmoid(-positive) * live[...]
    tail_grad[...] = pack(gpos * e)
    pull[...] = gpos * t + pulled[...]


def positive_terms(tail, hr, live, pulled):
    return pl.pallas_call(
        positives_body,
        grid=(GROUPS,),
        in_specs=[packed_block, grouped(D), grouped(1), grouped(D)],
        out_specs=[packed_block, grouped(D)],
        out_shape=[packed_rows, jax.ShapeDtypeStruct((SLOTS, D), f32)],
        compiler_params=params(),
        cost_estimate=cost(0.01, 16),
        name="positive_terms",
    )(tail, hr, live, pulled)


def relation_body(row, h, pull, out, hi, lo):
    @pl.when(pl.program_id(0) == 0)
    def _():
        hi[...], lo[...] = split(h[...] * pull[...])

    pick = picks_rows(row[...], BLOCK, BLOCK * pl.program_id(0))
    out[...] = nn(pick, hi[...]) + nn(pick, lo[...])


def relation_terms(row, h, pull):
    return pl.pallas_call(
        relation_body,
        grid=(RELS // BLOCK,),
        in_specs=[full((1, SLOTS)), full((SLOTS, D)), full((SLOTS, D))],
        out_specs=blocked(D),
        out_shape=jax.ShapeDtypeStruct((RELS, D), f32),
        scratch_shapes=[pltpu.VMEM((SLOTS, D), bf16), pltpu.VMEM((SLOTS, D), bf16)],
        compiler_params=params(),
        cost_estimate=cost(13, 16),
        name="relation_terms",
    )(row, h, pull)


def transposed(x):
    return jnp.concatenate([x, jnp.zeros((x.shape[0], 512 - D), f32)], axis=1).T[:D]


def head_body(column, r, pull, neg_column, neg, out, hi, lo):
    @pl.when(pl.program_id(0) == 0)
    def _():
        for s in range(STEPS):
            part = slice(s * BLOCK, (s + 1) * BLOCK)
            hi[:, part], lo[:, part] = split(transposed(r[part] * pull[part]))

    start = pl.program_id(0) * BLOCK
    pick = picks_lanes(column[...], BLOCK, start)
    neg_pick = picks_lanes(neg_column[...], BLOCK, start)
    neg_hi, neg_lo = split(neg[...])
    out[0] = nn(hi[...], pick) + nn(lo[...], pick) + tn(neg_hi, neg_pick) + tn(neg_lo, neg_pick)


def head_terms(column, r, pull, neg_column, neg):
    return pl.pallas_call(
        head_body,
        grid=(ENT_DEV // BLOCK,),
        in_specs=[full((SLOTS, 1)), full((SLOTS, D)), full((SLOTS, D)), full((OWN_NEG, 1)), full((OWN_NEG, D))],
        out_specs=pl.BlockSpec((1, D, BLOCK), lambda s: (s, 0, 0)),
        out_shape=jax.ShapeDtypeStruct((ENT_DEV // BLOCK, D, BLOCK), f32),
        scratch_shapes=[pltpu.VMEM((D, SLOTS), bf16), pltpu.VMEM((D, SLOTS), bf16)],
        compiler_params=params(),
        cost_estimate=cost(3, 10),
        name="head_terms",
    )(column, r, pull, neg_column, neg)


def tail_body(column, incoming, heads, out, hi, lo):
    @pl.when(pl.program_id(0) == 0)
    def _():
        for s in range(GROUPS):
            part = slice(s * GROUP_ROWS, (s + 1) * GROUP_ROWS)
            block = incoming[s * GROUP : (s + 1) * GROUP]
            hi[:, part], lo[:, part] = split(transposed(unpack(block)))

    pick = picks_lanes(column[...], BLOCK, pl.program_id(0) * BLOCK)
    out[0] = heads[0] + (nn(hi[...], pick) + nn(lo[...], pick))


def tail_terms(column, incoming, heads):
    chunk = pl.BlockSpec((1, D, BLOCK), lambda s: (s, 0, 0))
    return pl.pallas_call(
        tail_body,
        grid=(ENT_DEV // BLOCK,),
        in_specs=[full((SLOTS, 1)), full((ENT_PARTS, PACKED, 128)), chunk],
        out_specs=chunk,
        out_shape=jax.ShapeDtypeStruct((ENT_DEV // BLOCK, D, BLOCK), f32),
        scratch_shapes=[pltpu.VMEM((D, SLOTS), bf16), pltpu.VMEM((D, SLOTS), bf16)],
        compiler_params=params(),
        cost_estimate=cost(3, 8),
        name="tail_terms",
    )(column, incoming, heads)


def position():
    ent, y = lax.axis_index("ent"), lax.axis_index("rep")
    return lax.div(ent, NX * NC), lax.rem(lax.div(ent, NC), NX), lax.rem(ent, NC), y


def device(z, x, c, y):
    return ((z * NX + x) * NC + c, y)


def ahead(i, k, n):
    return lax.rem(i + k, n)


def along_z(k):
    z, x, c, y = position()
    return device(ahead(z, k, NZ), x, c, y)


def along_x(k):
    z, x, c, y = position()
    return device(z, ahead(x, k, NX), c, y)


def along_y(k):
    z, x, c, y = position()
    return device(z, x, c, ahead(y, k, NY))


def other_core():
    z, x, c, y = position()
    return device(z, x, 1 - c, y)


def meet(peers):
    barrier = pltpu.get_barrier_semaphore()
    for peer in peers:
        pl.semaphore_signal(barrier, inc=1, device_id=peer, device_id_type=MESH)
    pl.semaphore_wait(barrier, len(peers))


def send(src, dst, send_sem, recv_sem, peer):
    copy = pltpu.make_async_remote_copy(
        src_ref=src, dst_ref=dst, send_sem=send_sem, recv_sem=recv_sem, device_id=peer, device_id_type=MESH
    )
    copy.start()
    return copy


def first_exchange_body(tails, neg, table, asked, negs, own, send_sem, recv_sem, ask_send, ask_recv):
    z, x, c, y = position()
    ent = lax.axis_index("ent")

    def peer(k):
        return (lax.rem(ent + k, ENT_PARTS), y)

    barrier = pltpu.get_barrier_semaphore()

    def greet(k, carry):
        pl.semaphore_signal(barrier, inc=1, device_id=peer(k), device_id_type=MESH)
        return carry

    lax.fori_loop(1, ENT_PARTS, greet, 0)
    hi, lo = split(table[...])
    pick = picks_lanes(neg[...], ENT_DEV)
    own[...] = nt(pick, hi) + nt(pick, lo)
    pl.semaphore_wait(barrier, ENT_PARTS - 1)

    copies = [send(own, negs.at[c, x, z], send_sem.at[k], recv_sem.at[k], along_z(k)) for k in range(1, NZ)]

    def ask_copy(k):
        to, y_own = peer(k)
        return pltpu.make_async_remote_copy(
            src_ref=tails.at[to],
            dst_ref=asked.at[ent],
            send_sem=ask_send.at[k],
            recv_sem=ask_recv.at[k],
            device_id=(to, y_own),
            device_id_type=MESH,
        )

    def ask(k, carry):
        ask_copy(k).start()
        return carry

    def finish(k, carry):
        ask_copy(k).wait()
        return carry

    lax.fori_loop(1, ENT_PARTS, ask, 0)
    asked[ent] = tails[ent]
    negs[c, x, z] = own[...]
    for copy in copies:
        copy.wait()
    mine = negs.at[c, x]
    copies = [
        send(mine, mine, send_sem.at[NZ + k], recv_sem.at[NZ + k], along_x(k)) for k in range(1, NX)
    ]
    for copy in copies:
        copy.wait()
    mine = negs.at[c]
    copy = send(mine, mine, send_sem.at[0], recv_sem.at[0], other_core())
    lax.fori_loop(1, ENT_PARTS, finish, 0)
    copy.wait()


def first_exchange(tails, neg, table):
    space = pl.BlockSpec(memory_space=pltpu.VMEM)
    return pl.pallas_call(
        first_exchange_body,
        in_specs=[space] * 3,
        out_specs=[space] * 2,
        out_shape=[
            jax.ShapeDtypeStruct((ENT_PARTS, 1, 128), i32),
            jax.ShapeDtypeStruct((NC, NX, NZ, OWN_NEG, D), f32),
        ],
        scratch_shapes=[
            pltpu.VMEM((OWN_NEG, D), f32),
            pltpu.SemaphoreType.DMA((NZ + NX,)),
            pltpu.SemaphoreType.DMA((NZ + NX,)),
            pltpu.SemaphoreType.DMA((ENT_PARTS,)),
            pltpu.SemaphoreType.DMA((ENT_PARTS,)),
        ],
        compiler_params=params(collective_id=0),
        cost_estimate=cost(0, 40),
        name="first_exchange",
    )(tails, neg, table)


def sum_negatives_body(part, out, at_core, at_x, at_z, send_sem, recv_sem):
    z, x, c, y = position()
    meet([along_z(k) for k in range(1, NZ)] + [along_x(k) for k in range(1, NX)] + [other_core()])
    first = send(part.at[1 - c], at_core, send_sem.at[0], recv_sem.at[0], other_core())
    first.wait_recv()
    at_core[...] += part[c]
    copies = [
        send(at_core.at[ahead(x, k, NX)], at_x.at[k], send_sem.at[NZ + k], recv_sem.at[NZ + k], along_x(k))
        for k in range(1, NX)
    ]
    for copy in copies:
        copy.wait_recv()
    at_x[0] = at_core[x] + at_x[1] + at_x[2] + at_x[3]
    later = [
        send(at_x.at[0, ahead(z, k, NZ)], at_z.at[k], send_sem.at[k], recv_sem.at[k], along_z(k))
        for k in range(1, NZ)
    ]
    total = at_x[0, z]
    for k in range(1, NZ):
        later[k - 1].wait_recv()
        total += at_z[k]
    out[...] = total
    for copy in [first] + copies + later:
        copy.wait_send()


def sum_negatives(part):
    return pl.pallas_call(
        sum_negatives_body,
        in_specs=[pl.BlockSpec(memory_space=pltpu.VMEM)],
        out_specs=pl.BlockSpec(memory_space=pltpu.VMEM),
        out_shape=jax.ShapeDtypeStruct((OWN_NEG, D), f32),
        scratch_shapes=[
            pltpu.VMEM((NX, NZ, OWN_NEG, D), f32),
            pltpu.VMEM((NX, NZ, OWN_NEG, D), f32),
            pltpu.VMEM((NZ, OWN_NEG, D), f32),
            pltpu.SemaphoreType.DMA((NZ + NX,)),
            pltpu.SemaphoreType.DMA((NZ + NX,)),
        ],
        compiler_params=params(collective_id=1),
        cost_estimate=cost(0, 40),
        name="sum_negatives",
    )(part)


class Half:
    def __init__(self, dense, base, rows, m1, m2, along1, along2, acc, far, near, last, sems, first_sem):
        self.dense, self.base, self.rows, self.m1, self.m2 = dense, base, rows, m1, m2
        self.along1, self.along2 = along1, along2
        self.acc, self.far, self.near, self.last = acc, far, near, last
        self.sems, self.first_sem, self.copies = sems, first_sem, {}

    def chunk(self, core, o):
        start = self.base + (core * 4 + ahead(self.m1, o, 4)) * 4 * self.rows
        return pl.ds(pl.multiple_of(start, 8), 4 * self.rows)

    def start(self, name, src, dst, peer):
        index = self.first_sem + len(self.copies)
        self.copies[name] = send(src, dst, self.sems[0].at[index], self.sems[1].at[index], peer)

    def got(self, name):
        self.copies[name].wait_recv()

    def start_core(self, c):
        for o in (2, 1, 3, 0):
            self.start(("core", o), self.dense.at[self.chunk(1 - c, o)], self.acc.at[o], other_core())

    def add_core(self, c, o):
        self.got(("core", o))
        self.acc[o] += self.dense[self.chunk(c, o)]

    def ring_far(self, c):
        two = 2 * self.rows
        self.add_core(c, 2)
        self.start("far right", self.acc.at[2, :two], self.far.at[0], self.along1(1))
        self.start("far left", self.acc.at[2, two:], self.far.at[1], self.along1(3))

    def ring_early(self, c):
        two = 2 * self.rows
        self.add_core(c, 1)
        self.start("early right", self.acc.at[1, two:], self.near.at[0, two:], self.along1(1))
        self.add_core(c, 3)
        self.start("early left", self.acc.at[3, :two], self.near.at[1, :two], self.along1(3))
        self.add_core(c, 0)

    def ring_near(self):
        two = 2 * self.rows
        self.got("far right")
        self.acc[1, :two] += self.far[0]
        self.start("near right", self.acc.at[1, :two], self.near.at[0, :two], self.along1(1))
        self.got("far left")
        self.acc[3, two:] += self.far[1]
        self.start("near left", self.acc.at[3, two:], self.near.at[1, two:], self.along1(3))

    def second(self):
        for name in ("early right", "early left", "near right", "near left"):
            self.got(name)
        self.acc[0] += self.near[0] + self.near[1]
        for k in (2, 1, 3):
            part = pl.ds(pl.multiple_of(ahead(self.m2, k, 4) * self.rows, 8), self.rows)
            self.start(("second", k), self.acc.at[0, part], self.last.at[k], self.along2(k))

    def result(self):
        total = self.acc[0, pl.ds(pl.multiple_of(self.m2 * self.rows, 8), self.rows)]
        for k in (1, 3, 2):
            self.got(("second", k))
            total += self.last[k]
        return total

    def finish(self):
        for copy in self.copies.values():
            copy.wait_send()


def sum_relations_body(
    dense, out, acc_a, far_a, near_a, last_a, acc_b, far_b, near_b, last_b, going, arrived, send_sem, recv_sem
):
    z, x, c, y = position()
    meet(
        [along_z(k) for k in range(1, NZ)]
        + [along_x(k) for k in range(1, NX)]
        + [along_y(k) for k in range(1, NY)]
        + [other_core()]
    )
    sems = (send_sem, recv_sem)
    a = Half(dense, 0, ROWS_A, y, x, along_y, along_x, acc_a, far_a, near_a, last_a, sems, 0)
    b = Half(dense, BASE_B, ROWS_B, x, y, along_x, along_y, acc_b, far_b, near_b, last_b, sems, 16)
    a.start_core(c)
    b.start_core(c)
    a.ring_far(c)
    a.ring_early(c)
    b.ring_far(c)
    b.ring_early(c)
    a.ring_near()
    b.ring_near()
    b.second()
    a.second()
    sum_b = b.result()
    sum_a = a.result()
    for i in range(NZ):
        going[i, 0:8] = sum_a[8 * i : 8 * i + 8]
        going[i, 8:16] = sum_b[8 * i : 8 * i + 8]
        going[i, 16:20] = sum_a[8 * NZ + 4 * i : 8 * NZ + 4 * i + 4]
        going[i, 20:24] = jnp.zeros((4, D), f32)
    copies = [
        send(going.at[ahead(z, k, NZ)], arrived.at[k], send_sem.at[32 + k], recv_sem.at[32 + k], along_z(k))
        for k in range(1, NZ)
    ]
    total = going[z]
    for k in range(1, NZ):
        copies[k - 1].wait_recv()
        total += arrived[k]
    out[...] = total[:REL_DEV]
    a.finish()
    b.finish()
    for copy in copies:
        copy.wait_send()


def sum_relations(dense):
    def buffers(rows):
        return [
            pltpu.VMEM((4, 4 * rows, D), f32),
            pltpu.VMEM((2, 2 * rows, D), f32),
            pltpu.VMEM((2, 4 * rows, D), f32),
            pltpu.VMEM((4, rows, D), f32),
        ]

    return pl.pallas_call(
        sum_relations_body,
        in_specs=[pl.BlockSpec(memory_space=pltpu.VMEM)],
        out_specs=pl.BlockSpec(memory_space=pltpu.VMEM),
        out_shape=jax.ShapeDtypeStruct((REL_DEV, D), f32),
        scratch_shapes=buffers(ROWS_A)
        + buffers(ROWS_B)
        + [
            pltpu.VMEM((NZ, 24, D), f32),
            pltpu.VMEM((NZ, 24, D), f32),
            pltpu.SemaphoreType.DMA((32 + NZ,)),
            pltpu.SemaphoreType.DMA((32 + NZ,)),
        ],
        compiler_params=params(collective_id=2),
        cost_estimate=cost(0, 150),
        name="sum_relations",
    )(dense)


def sum_copies_body(part, out, far, near, send_sem, recv_sem):
    y = lax.axis_index("rep")
    right, left = along_y(1), along_y(3)
    meet([right, left])
    at = [ahead(y, o, 4) for o in range(4)]
    top, low = slice(0, D // 2), slice(D // 2, D)

    def start(index, src, dst, peer):
        return send(src, dst, send_sem.at[index], recv_sem.at[index], peer)

    def chunk(o, rows):
        return out.at[rows, pl.ds(pl.multiple_of(at[o] * BLOCK, BLOCK), BLOCK)]

    far_right = start(0, part.at[at[2], top], far.at[0], right)
    far_left = start(1, part.at[at[2], low], far.at[1], left)
    early_right = start(2, part.at[at[1], low], near.at[0, low], right)
    early_left = start(3, part.at[at[3], top], near.at[1, top], left)
    far_right.wait_recv()
    far[0] += part[at[1], top]
    near_right = start(4, far.at[0], near.at[0, top], right)
    far_left.wait_recv()
    far[1] += part[at[3], low]
    near_left = start(5, far.at[1], near.at[1, low], left)

    early_left.wait_recv()
    near_right.wait_recv()
    chunk(0, top)[...] = part[at[0], top] + near[0, top] + near[1, top]
    own_top_right = start(6, chunk(0, top), chunk(0, top), right)
    own_top_left = start(7, chunk(0, top), chunk(0, top), left)
    early_right.wait_recv()
    near_left.wait_recv()
    chunk(0, low)[...] = part[at[0], low] + near[0, low] + near[1, low]
    own_low_left = start(8, chunk(0, low), chunk(0, low), left)
    own_low_right = start(9, chunk(0, low), chunk(0, low), right)
    own_top_right.wait_recv()
    next_right = start(10, chunk(3, top), chunk(3, top), right)
    own_low_left.wait_recv()
    next_left = start(11, chunk(1, low), chunk(1, low), left)
    for copy in (own_top_left, own_low_right, next_right, next_left):
        copy.wait_recv()
    for copy in (far_right, far_left, early_right, early_left, near_right, near_left):
        copy.wait_send()
    for copy in (own_top_right, own_top_left, own_low_left, own_low_right, next_right, next_left):
        copy.wait_send()


def sum_copies(part):
    return pl.pallas_call(
        sum_copies_body,
        in_specs=[pl.BlockSpec(memory_space=pltpu.VMEM)],
        out_specs=pl.BlockSpec(memory_space=pltpu.VMEM),
        out_shape=jax.ShapeDtypeStruct((D, ENT_DEV), f32),
        scratch_shapes=[
            pltpu.VMEM((2, D // 2, BLOCK), f32),
            pltpu.VMEM((2, D, BLOCK), f32),
            pltpu.SemaphoreType.DMA((12,)),
            pltpu.SemaphoreType.DMA((12,)),
        ],
        compiler_params=params(collective_id=3),
        cost_estimate=cost(0, 80),
        name="sum_copies",
    )(part)


def place_edges(head_row, relation, tail_owner, tail_row, live_blocks):
    live = jnp.arange(EDGES_B, dtype=i32)[None, :] < SPAN * live_blocks[:, None]
    before = jnp.arange(EDGES_B)[None, :] < jnp.arange(EDGES_B)[:, None]
    same = tail_owner[:, :, None] == tail_owner[:, None, :]
    rank = jnp.sum((same & before[None]).astype(i32), axis=2)
    key = jnp.where(live, tail_owner * CAPACITY + rank, -1)
    slots = jnp.arange(ENT_PARTS * CAPACITY, dtype=i32)
    match = key[:, None, :] == slots[None, :, None]

    def placed(values):
        found = jnp.sum(jnp.where(match, values[:, None, :] + 1, 0), axis=2) - 1
        found = found.reshape(BUCKETS, ENT_PARTS, CAPACITY)
        return jnp.transpose(found, (1, 0, 2)).reshape(ENT_PARTS, PAIR)

    ends = placed(head_row * ENT_DEV + tail_row)
    taken = ends >= 0
    heads = jnp.where(taken, lax.shift_right_arithmetic(ends, 10), -1)
    tails = jnp.where(taken, ends & (ENT_DEV - 1), -1)
    return heads, placed(relation), tails


def dense_rows(rel):
    owner, j = rel // REL_DEV, rel % REL_DEV
    y, ent = owner % NY, owner // NY
    c, x, z = ent % NC, (ent // NC) % NX, ent // (NC * NX)
    in_a = (c * NY + y) * NX + x
    in_b = BASE_B + ((c * NX + x) * NY + y) * ROWS_B + z * 8 + j - 8
    row_a = in_a * ROWS_A + z * 8 + j
    row_c = in_a * ROWS_A + NZ * 8 + z * 4 + j - 16
    return jnp.where(rel < 0, -1, jnp.where(j < 8, row_a, jnp.where(j < 16, in_b, row_c)))


def shards(entity_table, relation_table, head_row, relation, tail_owner, tail_row, live_blocks, negative_row):
    table, rels = entity_table.T, relation_table.T
    heads, rel, tails = place_edges(
        head_row[0, 0], relation[0, 0], tail_owner[0, 0, :, :, 0], tail_row[0, 0], live_blocks[0, 0]
    )
    head_column = heads.reshape(SLOTS, 1)
    live = (head_column >= 0).astype(f32)
    neg_column = negative_row.reshape(OWN_NEG, 1)
    asked, negs = first_exchange(jnp.pad(tails, ((0, 0), (0, 128 - PAIR)))[:, None, :], neg_column, table)
    asked_column = asked[:, 0, :PAIR].reshape(SLOTS, 1)
    rows = gather_asked(asked_column, table)
    fetched = lax.all_to_all(rows, "ent", split_axis=0, concat_axis=0, tiled=True)
    h, r, hr = gather_heads(head_column, rel.reshape(SLOTS, 1), table, rels)
    pulled, pushed = negative_terms(hr, live, negs.reshape(NEG, D))
    neg_grad = sum_negatives(pushed.reshape(NC, NX, NZ, OWN_NEG, D))
    pulled, neg_grad = lax.optimization_barrier((pulled, neg_grad))
    tail_grad, pull = positive_terms(fetched, hr, live, pulled)
    incoming = lax.all_to_all(tail_grad, "ent", split_axis=0, concat_axis=0, tiled=True)
    dense = relation_terms(dense_rows(rel).reshape(1, SLOTS), h, pull)
    rel_grad = sum_relations(dense)
    pull, rel_grad = lax.optimization_barrier((pull, rel_grad))
    head_part = head_terms(head_column, r, pull, neg_column, neg_grad)
    incoming, head_part = lax.optimization_barrier((incoming, head_part))
    part = tail_terms(asked_column, incoming, head_part)
    return sum_copies(part).T, rel_grad


def solution(mesh):
    placed = (
        P("ent", None),
        P(),
        P("ent", "rep", None, None),
        P("ent", "rep", None, None),
        P("ent", "rep", None, None, None),
        P("ent", "rep", None, None),
        P("ent", "rep", None),
        P("ent"),
    )
    return jax.shard_map(
        shards,
        mesh=mesh,
        in_specs=placed,
        out_specs=(P("ent", None), P(("ent", "rep"), None)),
        check_vma=False,
    )
```
